512 devices in a mesh: chan: 64 (over y_hi, z, core), tm: 8 (over y_lo, x).
Axes of the slice: x: 4, y: 4 (y_hi: 2, y_lo: 2; y = y_hi * 2 + y_lo), z: 16, core: 2. Of those that a mesh axis runs over, the one named last changes fastest.
Arguments:
- voltages: bfloat16 [1024, 96, 8192], P('chan', 'tm'), may hold values from -0.9921875 to 0.9921875, as said below
- eq_gain: float32 [1024, 4096], P('chan'), may hold values from 0.5 to 2
Outputs:
- visibilities: float32 [2, 4096, 32, 1024], P(None, ('chan', 'tm'))
The draws below stay inside these ranges and needn't reach their ends.
Inputs may be any that keep to these rules, and one draw needn't show every extreme that they name: `voltages`: each sample is an integer of -127..127 divided by 128.
All inputs are finite; a program needn't handle non-finite values.
Results may differ from the reference program's by a relative error of at most 0.0078.
Values may be sent and summed in bfloat16 or wider, within the bound.
No kernel may reach another device: no remote copies, remote signals or barrier semaphores. Data moves between devices by JAX's collectives and lax.ppermute only.
A program may use at most 128 MiB of HBM per device.

```python
import math
import jax
import jax.numpy as jnp
import numpy as np
from jax import lax

N_IN = 1024
FFT_LEN = 8192
TAPS = 16
LA = 128
REF = 32
CH = 4096
SPECTRA = 96


def draw_voltages(key, part):
    key = jax.random.fold_in(key, 11)
    shape = (N_IN, SPECTRA, FFT_LEN)
    levels = jax.random.randint(key, shape, -127, 128, dtype=jnp.int32)
    values = levels.astype(jnp.float32) * (1.0 / 128.0)
    values = values.at[0, 0, 0].set(127.0 / 128.0)
    values = values.at[0, 0, 1].set(-127.0 / 128.0)
    return values.astype(jnp.bfloat16)


def shard_levels(own_key, shape, split, least, largest):
    factor_of = 1.0
    for position, shards_of in split:
        steps = jax.random.uniform(jax.random.fold_in(jax.random.fold_in(own_key, 6), position), (shards_of,), jnp.float32, least / len(split), largest / len(split))
        factor_of = factor_of * jnp.repeat(jnp.exp(steps), shape[position] // shards_of).reshape((-1,) + (1,) * (len(shape) - 1 - position))
    return factor_of


def setup_inputs(seed: int = 0) -> dict:
    streams_of = jax.random.split(jax.random.key(seed), 3)
    voltages = draw_voltages(jax.random.fold_in(streams_of[2], 71), 0)
    eq_gain = jnp.clip(jnp.exp(math.log(2.0) - 1.3862944 * jax.random.uniform(streams_of[1], (N_IN, CH), jnp.float32) ** shard_levels(streams_of[1], (N_IN, CH), ((0, 64),), -0.2, 0.2)), 0.5, 2.0)
    return dict(voltages=voltages, eq_gain=eq_gain)


def make_tables(length, inner, taps_count):
    outer_len = length // inner
    outer_row = np.arange(outer_len)
    angle_one = 2.0 * np.pi * np.outer(outer_row, outer_row) / outer_len
    first_table = jnp.asarray(np.concatenate([np.cos(angle_one), -np.sin(angle_one)], axis=1), jnp.float32).astype(jnp.bfloat16)
    inner_row = np.arange(inner)
    angle_twist = 2.0 * np.pi * np.outer(outer_row, inner_row) / length
    twist_cos = jnp.asarray(np.cos(angle_twist), jnp.float32)
    twist_sin = jnp.asarray(np.sin(angle_twist), jnp.float32)
    half_row = np.arange(inner // 2)
    angle_two = 2.0 * np.pi * np.outer(inner_row, half_row) / inner
    upper_rows = np.concatenate([np.cos(angle_two), -np.sin(angle_two)], axis=1)
    lower_rows = np.concatenate([np.sin(angle_two), np.cos(angle_two)], axis=1)
    second_table = jnp.asarray(np.concatenate([upper_rows, lower_rows], axis=0), jnp.float32).astype(jnp.bfloat16)
    sample_pos = np.arange(taps_count * length)
    sinc_arg = np.pi * (sample_pos - taps_count * length / 2 + 0.5) / length
    proto = np.sin(sinc_arg) / sinc_arg
    proto = proto * (0.5 - 0.5 * np.cos(2.0 * np.pi * (sample_pos + 0.5) / (taps_count * length)))
    proto = proto / np.sqrt(np.mean(proto ** 2) * taps_count)
    tap_table = jnp.asarray(proto.reshape(taps_count, length)[::-1].copy(), jnp.float32)
    return (first_table, twist_cos, twist_sin, second_table, tap_table)

def spectra_block(raw, gains, tables):
    first_table, twist_cos, twist_sin, second_table, tap_table = tables
    taps_count = tap_table.shape[0]
    group_size, count = (raw.shape[0], raw.shape[1])
    samples = raw.astype(jnp.float32)
    length = samples.shape[-1]
    padding = jnp.zeros((group_size, taps_count - 1, length), jnp.float32)
    samples = jnp.concatenate([padding, samples], axis=1)
    filtered = tap_table[0] * samples[:, taps_count - 1:taps_count - 1 + count]
    for lag in range(1, taps_count):
        filtered = filtered + tap_table[lag] * samples[:, taps_count - 1 - lag:taps_count - 1 - lag + count]
    filtered = filtered.astype(jnp.bfloat16)
    outer_len = first_table.shape[0]
    inner = twist_cos.shape[1]
    shaped = filtered.reshape(group_size, count, outer_len, inner).astype(jnp.float32)
    section_one = jnp.einsum('gsba,bc->gsca', shaped, first_table.astype(jnp.float32), precision=lax.Precision.HIGHEST)
    real_one = section_one[:, :, :outer_len]
    imag_one = section_one[:, :, outer_len:]
    turned_real = real_one * twist_cos + imag_one * twist_sin
    turned_imag = imag_one * twist_cos - real_one * twist_sin
    turned = jnp.concatenate([turned_real, turned_imag], axis=-1).astype(jnp.bfloat16)
    section_two = jnp.einsum('gskj,jm->gsmk', turned.astype(jnp.float32), second_table.astype(jnp.float32), precision=lax.Precision.HIGHEST)
    half = inner // 2
    scaled_gain = gains * (1.0 / math.sqrt(length))
    real_part = (section_two[:, :, :half].reshape(group_size, count, -1) * scaled_gain[:, None, :]).astype(jnp.bfloat16)
    imag_part = (section_two[:, :, half:].reshape(group_size, count, -1) * scaled_gain[:, None, :]).astype(jnp.bfloat16)
    return (real_part, imag_part)

def correlate(real_part, imag_part, ref_real, ref_imag, inverse_count):
    real_f = real_part.astype(jnp.float32)
    imag_f = imag_part.astype(jnp.float32)
    rref_f = ref_real.astype(jnp.float32)
    iref_f = ref_imag.astype(jnp.float32)
    high = lax.Precision.HIGHEST
    real_real = jnp.einsum('itc,rtc->cri', real_f, rref_f, precision=high)
    imag_imag = jnp.einsum('itc,rtc->cri', imag_f, iref_f, precision=high)
    imag_real = jnp.einsum('itc,rtc->cri', imag_f, rref_f, precision=high)
    real_imag = jnp.einsum('itc,rtc->cri', real_f, iref_f, precision=high)
    return ((real_real + imag_imag) * inverse_count, (imag_real - real_imag) * inverse_count)

def reference(voltages, eq_gain):
    tables = make_tables(FFT_LEN, LA, TAPS)
    ref_real, ref_imag = spectra_block(voltages[:REF], eq_gain[:REF], tables)
    group_size = math.gcd(N_IN, 16)
    count_groups = N_IN // group_size
    inverse_count = 1.0 / SPECTRA

    def one_group(pair):
        real_part, imag_part = spectra_block(pair[0], pair[1], tables)
        return correlate(real_part, imag_part, ref_real, ref_imag, inverse_count)
    grouped_raw = voltages.reshape(count_groups, group_size, SPECTRA, voltages.shape[-1])
    grouped_gain = eq_gain.reshape(count_groups, group_size, CH)
    vis_real, vis_imag = lax.map(one_group, (grouped_raw, grouped_gain))
    vis_real = vis_real.transpose(1, 2, 0, 3).reshape(CH, REF, N_IN)
    vis_imag = vis_imag.transpose(1, 2, 0, 3).reshape(CH, REF, N_IN)
    return jnp.stack([vis_real, vis_imag])
```

```python
import math

import jax
import jax.numpy as jnp
import numpy as np
from jax import lax
from jax.experimental import pallas as pl
from jax.experimental.pallas import tpu as pltpu
from jax.sharding import Mesh, PartitionSpec as P

FFT_LEN = 8192
TAPS = 16
LA = 128
REF = 32
OUTER = FFT_LEN // LA
SPECTRA = 96
STEP = 16
LEAD = 16
VMEM = 56 * 1024 * 1024


def make_tables():
    outer_row = np.arange(OUTER)
    angle_one = 2.0 * np.pi * np.outer(outer_row, outer_row) / OUTER
    first_table = np.concatenate([np.cos(angle_one), -np.sin(angle_one)], axis=1)
    inner_row = np.arange(LA)
    angle_twist = 2.0 * np.pi * np.outer(outer_row, inner_row) / FFT_LEN
    half_row = np.arange(LA // 2)
    angle_two = 2.0 * np.pi * np.outer(inner_row, half_row) / LA
    upper_rows = np.concatenate([np.cos(angle_two), -np.sin(angle_two)], axis=1)
    lower_rows = np.concatenate([np.sin(angle_two), np.cos(angle_two)], axis=1)
    second_table = np.concatenate([upper_rows, lower_rows], axis=0)
    second_table = second_table.reshape(2 * LA, 2, 32, 2).transpose(0, 3, 1, 2).reshape(2 * LA, LA)
    sample_pos = np.arange(TAPS * FFT_LEN)
    sinc_arg = np.pi * (sample_pos - TAPS * FFT_LEN / 2 + 0.5) / FFT_LEN
    proto = np.sin(sinc_arg) / sinc_arg
    proto = proto * (0.5 - 0.5 * np.cos(2.0 * np.pi * (sample_pos + 0.5) / (TAPS * FFT_LEN)))
    proto = proto / np.sqrt(np.mean(proto**2) * TAPS)
    taps = proto.reshape(TAPS, FFT_LEN)[::-1].reshape(TAPS, OUTER, LA)
    return (
        jnp.asarray(first_table.T, jnp.float32).astype(jnp.bfloat16),
        jnp.asarray(np.cos(angle_twist), jnp.float32),
        jnp.asarray(np.sin(angle_twist), jnp.float32),
        jnp.asarray(second_table, jnp.float32).astype(jnp.bfloat16),
        jnp.asarray(taps, jnp.float32),
    )


def frames_kernel(x_ref, o_ref, wide):
    for b in range(OUTER):
        wide[pl.ds(16 * b, 16), :] = x_ref[0, :, b * LA : (b + 1) * LA].astype(jnp.float32)
    for i in range(16):
        for h in range(4):
            rows = wide[pl.ds(256 * h + i, 16, stride=16), :]
            o_ref[i // 2, i % 2, 0, h * 16 : (h + 1) * 16, :] = rows.astype(jnp.bfloat16)


def to_frames(by_time):
    times, inputs, _ = by_time.shape
    return pl.pallas_call(
        frames_kernel,
        grid=(times,),
        in_specs=[pl.BlockSpec((1, inputs, FFT_LEN), lambda s: (s, 0, 0))],
        out_specs=pl.BlockSpec((8, 2, 1, OUTER, LA), lambda s: (0, 0, s, 0, 0)),
        out_shape=jax.ShapeDtypeStruct((8, 2, times, OUTER, LA), jnp.bfloat16),
        scratch_shapes=[pltpu.VMEM((inputs * OUTER, LA), jnp.float32)],
        compiler_params=pltpu.CompilerParams(vmem_limit_bytes=VMEM),
        name="frames",
    )(by_time)


def spectra_kernel(x_ref, gain_ref, first_ref, cos_ref, sin_ref, second_ref, taps_ref, o_ref, held, filt, spec):
    chunk = pl.program_id(0)

    @pl.when(chunk == 0)
    def _():
        for i in range(2):
            held[i, 0:LEAD] = jnp.zeros((LEAD, OUTER, LA), jnp.bfloat16)
            for t in range(8):
                held[i, LEAD + 12 * t : LEAD + 12 * t + 12] = x_ref[t, i]

    base = chunk * STEP

    def filter_step(n, carry):
        i = n // 4
        row = pl.multiple_of((n % 4) * 16, 16)
        for group in range(STEP // 8):
            acc = [None] * 8
            for m in range(8 + TAPS - 1):
                v = held[i, base + (LEAD - TAPS + 1) + group * 8 + m, pl.ds(row, 16), :].astype(jnp.float32)
                for j in range(8):
                    p = j + TAPS - 1 - m
                    if 0 <= p < TAPS:
                        term = taps_ref[p, pl.ds(row, 16), :] * v
                        acc[j] = term if acc[j] is None else acc[j] + term
            for j in range(8):
                filt[i * (STEP // 4) + group * 2 + j // 4, pl.ds(row, 16), (j % 4) * LA : (j % 4 + 1) * LA] = acc[
                    j
                ].astype(jnp.bfloat16)
        return carry

    lax.fori_loop(0, 8, filter_step, 0)

    first = first_ref[...]
    second = second_ref[...]

    def transform_step(g, carry):
        i = g // (STEP // 4)
        part = jnp.dot(first, filt[g], preferred_element_type=jnp.float32)
        cos = cos_ref[...]
        sin = sin_ref[...]
        rows = []
        for f in range(4):
            u = part[:OUTER, f * LA : (f + 1) * LA]
            v = part[OUTER:, f * LA : (f + 1) * LA]
            rows.append(jnp.concatenate([u * cos + v * sin, v * cos - u * sin], axis=1).astype(jnp.bfloat16))
        turned = jnp.concatenate(rows, axis=0)
        whole = jnp.dot(turned, second, preferred_element_type=jnp.float32)
        gain = gain_ref[i]
        for f in range(4):
            spec[i, pl.ds(((g % (STEP // 4)) * 4 + f) * OUTER, OUTER), :] = whole[f * OUTER : (f + 1) * OUTER] * gain
        return carry

    lax.fori_loop(0, 2 * (STEP // 4), transform_step, 0)

    low = lax.broadcasted_iota(jnp.int32, (STEP, LA), 1) < LA // 2
    for k in range(OUTER):
        y0 = spec[0, pl.ds(k, STEP, stride=OUTER), :]
        y1 = spec[1, pl.ds(k, STEP, stride=OUTER), :]
        o_ref[0, k // 8, k % 8] = jnp.where(low, y0, pltpu.roll(y1, LA // 2, 1)).astype(jnp.bfloat16)
        o_ref[1, k // 8, k % 8] = jnp.where(low, pltpu.roll(y0, LA // 2, 1), y1).astype(jnp.bfloat16)


def spectra(framed, gain, tables):
    whole = lambda *shape: pl.BlockSpec(shape, lambda s: (0,) * len(shape))
    return pl.pallas_call(
        spectra_kernel,
        grid=(SPECTRA // STEP,),
        in_specs=[
            whole(8, 2, 12, OUTER, LA),
            whole(2, OUTER, LA),
            whole(LA, OUTER),
            whole(OUTER, LA),
            whole(OUTER, LA),
            whole(2 * LA, LA),
            whole(TAPS, OUTER, LA),
        ],
        out_specs=pl.BlockSpec((2, 8, 8, STEP, LA), lambda s: (0, 0, 0, s, 0)),
        out_shape=jax.ShapeDtypeStruct((2, 8, 8, SPECTRA, LA), jnp.bfloat16),
        scratch_shapes=[
            pltpu.VMEM((2, LEAD + SPECTRA, OUTER, LA), jnp.bfloat16),
            pltpu.VMEM((2 * (STEP // 4), OUTER, 4 * LA), jnp.bfloat16),
            pltpu.VMEM((2, STEP * OUTER, LA), jnp.float32),
        ],
        compiler_params=pltpu.CompilerParams(vmem_limit_bytes=VMEM),
        name="spectra",
    )(framed, gain, *tables)


def cross_kernel(x_ref, r_ref, o_ref, tx, tr):
    pad = jnp.zeros((LA - SPECTRA, LA), jnp.float32)
    for half in range(2):
        for s in range(16):
            for src, dst in ((x_ref, tx), (r_ref, tr)):
                block = jnp.concatenate([src[s, half].astype(jnp.float32), pad], axis=0)
                dst[half, pl.ds(s * LA, LA), :] = block.T

    def channel(q, carry):
        parts = []
        for half in range(2):
            xr = tx[half, pl.ds(q, 32, stride=64), :].astype(jnp.bfloat16)
            xi = tx[half, pl.ds(q + 32, 32, stride=64), :].astype(jnp.bfloat16)
            rr = tr[half, pl.ds(q, 32, stride=64), :].astype(jnp.bfloat16)
            ri = tr[half, pl.ds(q + 32, 32, stride=64), :].astype(jnp.bfloat16)
            left = jnp.concatenate([xr, xi], axis=1)
            right = jnp.concatenate(
                [jnp.concatenate([rr, ri], axis=1), jnp.concatenate([-ri, rr], axis=1)], axis=0
            )
            parts.append(
                lax.dot_general(left, right, (((1,), (1,)), ((), ())), preferred_element_type=jnp.float32)
            )
        both = jnp.concatenate(parts, axis=1) * (1.0 / SPECTRA)
        o_ref[q, 0] = both.astype(jnp.bfloat16)
        return carry

    lax.fori_loop(0, 32, channel, 0)


def cross(own, refs):
    block = pl.BlockSpec((16, 2, SPECTRA, LA), lambda r: (0, r, 0, 0))
    return pl.pallas_call(
        cross_kernel,
        grid=(4,),
        in_specs=[block, block],
        out_specs=pl.BlockSpec((32, 1, 32, LA), lambda r: (0, r, 0, 0)),
        out_shape=jax.ShapeDtypeStruct((32, 4, 32, LA), jnp.bfloat16),
        scratch_shapes=[pltpu.VMEM((2, 16 * LA, LA), jnp.float32)] * 2,
        compiler_params=pltpu.CompilerParams(vmem_limit_bytes=VMEM),
        name="cross",
    )(own, refs)


def turn_kernel(x_ref, o_ref):
    for n in range(8):
        block = jnp.concatenate([x_ref[4 * n + m, 0] for m in range(4)], axis=0).astype(jnp.float32).T
        for r in range(2):
            for part in range(2):
                o_ref[part, r, :, n * LA : (n + 1) * LA] = block[r * 64 + part * 32 : r * 64 + part * 32 + 32]


def turn(pieces):
    return pl.pallas_call(
        turn_kernel,
        grid=(4,),
        in_specs=[pl.BlockSpec((32, 1, 32, LA), lambda r: (0, r, 0, 0))],
        out_specs=pl.BlockSpec((2, 2, REF, 1024), lambda r: (0, r, 0, 0)),
        out_shape=jax.ShapeDtypeStruct((2, 8, REF, 1024), jnp.float32),
        compiler_params=pltpu.CompilerParams(vmem_limit_bytes=VMEM),
        name="turn",
    )(pieces)


def shards(voltages, eq_gain):
    tables = make_tables()
    frames = to_frames(jnp.swapaxes(voltages, 0, 1))
    framed = lax.all_to_all(frames, ("yl", "x"), 0, 0, tiled=True)
    mine = lax.axis_index("yl") * 4 + lax.axis_index("x")
    gain = lax.dynamic_slice(eq_gain, (2 * mine, 0), (2, eq_gain.shape[1])) * (1.0 / math.sqrt(FFT_LEN))
    gain = gain.reshape(2, 32, 2, OUTER).transpose(0, 3, 2, 1)
    gain = jnp.stack([gain, gain], axis=3).reshape(2, OUTER, LA)
    spec = spectra(framed, gain, tables)
    own = lax.all_to_all(spec.reshape(16, 8, SPECTRA, LA), ("core", "yl", "x"), 0, 0, tiled=True)
    first = (lax.axis_index("yh") == 0) & (lax.axis_index("z") == 0)
    refs = lax.psum(jnp.where(first, own, jnp.zeros_like(own)), ("yh", "z"))
    pieces = cross(own, refs)
    pieces = lax.all_to_all(pieces, ("yh", "z"), 0, 0, tiled=True)
    return turn(pieces)


def solution(mesh):
    fine = Mesh(mesh.devices.reshape(2, 16, 2, 2, 4), ("yh", "z", "core", "yl", "x"))
    chan, tm = ("yh", "z", "core"), ("yl", "x")
    return jax.shard_map(
        shards,
        mesh=fine,
        in_specs=(P(chan, tm, None), P(chan, None)),
        out_specs=P(None, chan + tm, None, None),
        check_vma=False,
    )
```

```python
import math

import jax
import jax.numpy as jnp
import numpy as np
from jax import lax
from jax.experimental import pallas as pl
from jax.experimental.pallas import tpu as pltpu
from jax.sharding import Mesh, PartitionSpec as P

FFT_LEN = 8192
TAPS = 16
LA = 128
HALF = LA // 2
REF = 32
OUTER = FFT_LEN // LA
SPECTRA = 96
HEAD = 64
TAIL = SPECTRA - HEAD
LEAD = 16
VMEM = 40 * 1024 * 1024


def make_tables():
    outer_row = np.arange(OUTER)
    angle_one = 2.0 * np.pi * np.outer(outer_row, outer_row) / OUTER
    first_table = np.concatenate([np.cos(angle_one), -np.sin(angle_one)], axis=1)
    inner_row = np.arange(LA)
    angle_twist = 2.0 * np.pi * np.outer(outer_row, inner_row) / FFT_LEN
    half_row = np.arange(HALF)
    angle_two = 2.0 * np.pi * np.outer(inner_row, half_row) / LA
    upper_rows = np.concatenate([np.cos(angle_two), -np.sin(angle_two)], axis=1)
    lower_rows = np.concatenate([np.sin(angle_two), np.cos(angle_two)], axis=1)
    second_table = np.concatenate([upper_rows, lower_rows], axis=0)
    second_table = second_table.reshape(2 * LA, 2, 2, 16, 2).transpose(0, 1, 3, 2, 4).reshape(2 * LA, 2, HALF)
    second_tables = np.stack([second_table.reshape(2 * LA, LA), second_table[:, ::-1].reshape(2 * LA, LA)])
    sample_pos = np.arange(TAPS * FFT_LEN)
    sinc_arg = np.pi * (sample_pos - TAPS * FFT_LEN / 2 + 0.5) / FFT_LEN
    proto = np.sin(sinc_arg) / sinc_arg
    proto = proto * (0.5 - 0.5 * np.cos(2.0 * np.pi * (sample_pos + 0.5) / (TAPS * FFT_LEN)))
    proto = proto / np.sqrt(np.mean(proto**2) * TAPS)
    taps = proto.reshape(TAPS, FFT_LEN)[::-1].reshape(TAPS, OUTER, LA)
    return (
        jnp.asarray(first_table.T, jnp.float32).astype(jnp.bfloat16),
        jnp.asarray(np.cos(angle_twist), jnp.float32),
        jnp.asarray(np.sin(angle_twist), jnp.float32),
        jnp.asarray(second_tables, jnp.float32).astype(jnp.bfloat16),
        jnp.asarray(taps, jnp.float32),
    )


def frames_kernel(x_ref, o0_ref, o1_ref, wide):
    for b in range(OUTER):
        wide[pl.ds(16 * b, 16), :] = x_ref[0, :, b * LA : (b + 1) * LA].astype(jnp.float32)
    for i in range(16):
        out = (o0_ref, o1_ref)[i % 2]
        for h in range(4):
            rows = wide[pl.ds(256 * h + i, 16, stride=16), :]
            out[i // 2, 0, h * 16 : (h + 1) * 16, :] = rows.astype(jnp.bfloat16)


def to_frames(by_time):
    times, inputs, _ = by_time.shape
    shape = jax.ShapeDtypeStruct((8, times, OUTER, LA), jnp.bfloat16)
    spec = pl.BlockSpec((8, 1, OUTER, LA), lambda s: (0, s, 0, 0))
    return pl.pallas_call(
        frames_kernel,
        grid=(times,),
        in_specs=[pl.BlockSpec((1, inputs, FFT_LEN), lambda s: (s, 0, 0))],
        out_specs=[spec, spec],
        out_shape=[shape, shape],
        scratch_shapes=[pltpu.VMEM((inputs * OUTER, LA), jnp.float32)],
        compiler_params=pltpu.CompilerParams(vmem_limit_bytes=VMEM),
        name="frames",
    )(by_time)


def filter_frames(x_ref, taps_ref, held, filt):
    held[0:LEAD] = jnp.zeros((LEAD, OUTER, LA), jnp.bfloat16)
    for t in range(8):
        held[LEAD + 12 * t : LEAD + 12 * t + 12] = x_ref[t]

    def step(n, carry):
        row = pl.multiple_of((n % 4) * 16, 16)
        base = (n // 4) * 8
        acc = [None] * 8
        for m in range(8 + TAPS - 1):
            v = held[base + (LEAD - TAPS + 1) + m, pl.ds(row, 16), :].astype(jnp.float32)
            for j in range(8):
                p = j + TAPS - 1 - m
                if 0 <= p < TAPS:
                    term = taps_ref[p, pl.ds(row, 16), :] * v
                    acc[j] = term if acc[j] is None else acc[j] + term
        for j in range(8):
            filt[(n // 4) * 2 + j // 4, pl.ds(row, 16), (j % 4) * LA : (j % 4 + 1) * LA] = acc[j].astype(jnp.bfloat16)
        return carry

    lax.fori_loop(0, 4 * SPECTRA // 8, step, 0)


def transform_frames(gain_ref, first_ref, cos_ref, sin_ref, second_ref, filt, spec):
    first = first_ref[...]

    def step(g, carry):
        part = jnp.dot(first, filt[g], preferred_element_type=jnp.float32)
        cos = cos_ref[...]
        sin = sin_ref[...]
        rows = []
        for f in range(4):
            u = part[:OUTER, f * LA : (f + 1) * LA]
            v = part[OUTER:, f * LA : (f + 1) * LA]
            rows.append(jnp.concatenate([u * cos + v * sin, v * cos - u * sin], axis=1).astype(jnp.bfloat16))
        for h in range(2):
            turned = jnp.concatenate([row[h * 32 : h * 32 + 32] for row in rows], axis=0)
            whole = jnp.dot(turned, second_ref[h], preferred_element_type=jnp.float32)
            gain = gain_ref[h * 32 : h * 32 + 32]
            for f in range(4):
                start = pl.multiple_of((g * 4 + f) * OUTER + h * 32, 32)
                spec[pl.ds(start, 32), :] = whole[f * 32 : f * 32 + 32] * gain
        return carry

    lax.fori_loop(0, SPECTRA // 4, step, 0)


def turn_spectra(t4, spec, head, tail, tail_row):
    low = lax.broadcasted_iota(jnp.int32, (LA, LA), 1) < HALF
    low_all = lax.broadcasted_iota(jnp.int32, (SPECTRA, LA), 1) < HALF
    low_half = lax.broadcasted_iota(jnp.int32, (HALF, LA), 1) < HALF
    for rp in range(4):
        tails = []
        for kp in range(2):
            k = t4 * 8 + rp * 2 + kp
            one = spec[pl.ds(k, SPECTRA, stride=OUTER), :]
            two = spec[pl.ds(k + 32, SPECTRA, stride=OUTER), :]
            re = jnp.where(low_all, one, two)
            im = jnp.where(low_all, two, one)
            whole = jnp.concatenate([re[:HEAD], im[:HEAD]], axis=0).T
            for k2 in range(2):
                start = (k2 * 8 + rp * 2 + kp) * HALF
                head[start : start + HALF, :] = jnp.where(
                    low_half, whole[k2 * HALF : k2 * HALF + HALF], whole[HALF - k2 * HALF : LA - k2 * HALF]
                )
            tails += [re[HEAD:], im[HEAD:]]
        whole = jnp.concatenate(tails, axis=0).T
        lane = lax.broadcasted_iota(jnp.int32, (HALF, LA), 1)
        real = (lane // TAIL) % 2 == 0
        for k2 in range(2):
            start = (k2 * 8 + tail_row + rp) * HALF
            tail[start : start + HALF, :] = jnp.where(
                real, whole[k2 * HALF : k2 * HALF + HALF], whole[HALF - k2 * HALF : LA - k2 * HALF]
            )


def spread(t4, groups, o_ref):
    for k2 in range(2):
        for q in range(HALF):
            rows = [group[pl.ds(k2 * 8 * HALF + q, 8, stride=HALF), :] for group in groups]
            o_ref[q // 4, (q % 4) * 8 + k2 * 4 + t4] = jnp.concatenate(rows, axis=0).astype(jnp.bfloat16)


def spectra_first_kernel(
    x_ref, gain_ref, first_ref, cos_ref, sin_ref, second_ref, taps_ref, head_ref, kept_ref, held, filt, spec, head, tail
):
    filter_frames(x_ref, taps_ref, held, filt)
    transform_frames(gain_ref, first_ref, cos_ref, sin_ref, second_ref, filt, spec)

    def step(t4, carry):
        turn_spectra(t4, spec, head, tail, 0)
        spread(t4, [head], head_ref)
        for k2 in range(2):
            kept_ref[t4, k2] = tail[k2 * 8 * HALF : (k2 * 8 + 4) * HALF, :].astype(jnp.bfloat16)
        return carry

    lax.fori_loop(0, 4, step, 0)


def spectra_second_kernel(
    x_ref, gain_ref, first_ref, cos_ref, sin_ref, second_ref, taps_ref, kept_ref, o_ref, held, filt, spec, head, tail
):
    filter_frames(x_ref, taps_ref, held, filt)
    transform_frames(gain_ref, first_ref, cos_ref, sin_ref, second_ref, filt, spec)

    def step(t4, carry):
        turn_spectra(t4, spec, head, tail, 4)
        for k2 in range(2):
            tail[k2 * 8 * HALF : (k2 * 8 + 4) * HALF, :] = kept_ref[t4, k2].astype(jnp.float32)
        spread(t4, [head, tail], o_ref)
        return carry

    lax.fori_loop(0, 4, step, 0)


def spectra(framed, gain, tables, kept=None):
    first = kept is None
    out = jax.ShapeDtypeStruct((16, 32, 8 if first else 16, LA), jnp.bfloat16)
    keep = jax.ShapeDtypeStruct((4, 2, 4 * HALF, LA), jnp.bfloat16)
    return pl.pallas_call(
        spectra_first_kernel if first else spectra_second_kernel,
        out_shape=[out, keep] if first else out,
        scratch_shapes=[
            pltpu.VMEM((LEAD + SPECTRA, OUTER, LA), jnp.bfloat16),
            pltpu.VMEM((SPECTRA // 4, OUTER, 4 * LA), jnp.bfloat16),
            pltpu.VMEM((SPECTRA * OUTER, LA), jnp.float32),
            pltpu.VMEM((16 * HALF, LA), jnp.float32),
            pltpu.VMEM((16 * HALF, LA), jnp.float32),
        ],
        compiler_params=pltpu.CompilerParams(vmem_limit_bytes=VMEM),
        cost_estimate=pl.CostEstimate(flops=2_000_000_000, bytes_accessed=4_000_000, transcendentals=0),
        name="spectra_first" if first else "spectra_second",
    )(framed, gain, *tables, *(() if first else (kept,)))


def cross_kernel(first_ref, second_ref, o_ref, head, tail):
    def place(z, carry):
        for s in range(32):
            at = (s // 16) * 256 + (s % 16) + z * 16
            head[pl.ds(pl.multiple_of(at * 16, 16), 8), :] = first_ref[z, s].astype(jnp.float32)
            head[pl.ds(pl.multiple_of(at * 16 + 8, 8), 8), :] = second_ref[z, s, 0:8].astype(jnp.float32)
            tail[pl.ds(pl.multiple_of(at * 8, 8), 8), :] = second_ref[z, s, 8:16].astype(jnp.float32)
        return carry

    lax.fori_loop(0, 16, place, 0)
    lane = lax.broadcasted_iota(jnp.int32, (REF, LA), 1)
    head_sign = jnp.where(lane < HALF, -1.0, 1.0)
    tail_real = (lane // TAIL) % 2 == 0
    tail_sign = jnp.where(tail_real, -1.0, 1.0)
    for r in range(8):
        mine = lane // HALF == r % 2
        ref_head = head[pl.ds(r, REF, stride=8), :]
        ref_tail = jnp.where(mine, tail[pl.ds(r // 2, REF, stride=4), :], 0.0)
        im_head = pltpu.roll(ref_head, HALF, 1) * head_sign
        im_tail = jnp.where(tail_real, pltpu.roll(ref_tail, LA - TAIL, 1), pltpu.roll(ref_tail, TAIL, 1)) * tail_sign
        weights = jnp.concatenate(
            [jnp.concatenate([ref_head, ref_tail], axis=1), jnp.concatenate([im_head, im_tail], axis=1)], axis=0
        ).astype(jnp.bfloat16)
        for c in range(4):
            rows = jnp.concatenate(
                [
                    head[pl.ds(c * 256 * 8 + r, 256, stride=8), :].astype(jnp.bfloat16),
                    tail[pl.ds(c * 256 * 4 + r // 2, 256, stride=4), :].astype(jnp.bfloat16),
                ],
                axis=1,
            )
            part = lax.dot_general(weights, rows, (((1,), (1,)), ((), ())), preferred_element_type=jnp.float32)
            part = part * (1.0 / SPECTRA)
            for n in range(2):
                o_ref[n, r, :, c * 256 : (c + 1) * 256] = part[n * REF : (n + 1) * REF]


def cross(first, second):
    return pl.pallas_call(
        cross_kernel,
        out_shape=jax.ShapeDtypeStruct((2, 8, REF, 1024), jnp.float32),
        scratch_shapes=[pltpu.VMEM((1024 * 8, LA), jnp.float32), pltpu.VMEM((512 * 8, LA), jnp.float32)],
        compiler_params=pltpu.CompilerParams(vmem_limit_bytes=VMEM),
        cost_estimate=pl.CostEstimate(flops=500_000_000, bytes_accessed=5_000_000, transcendentals=0),
        name="cross",
    )(first, second)


def share(spec):
    rows = spec.shape[2]
    flat = lax.all_to_all(spec.reshape(512, rows, LA), ("z", "yh", "core", "yl", "x"), 0, 0, tiled=True)
    return flat.reshape(16, 32, rows, LA)


def after(value, other):
    return lax.optimization_barrier((value, other))[0]


def shards(voltages, eq_gain):
    tables = make_tables()
    mine = lax.axis_index("yl") * 4 + lax.axis_index("x")
    gain = lax.dynamic_slice(eq_gain, (2 * mine, 0), (2, eq_gain.shape[1])) * (1.0 / math.sqrt(FFT_LEN))
    gain = gain.reshape(2, 2, 16, 2, OUTER).transpose(0, 4, 2, 1, 3).reshape(2, OUTER, HALF)
    gain = jnp.concatenate([gain, gain], axis=2)
    frames0, frames1 = to_frames(jnp.swapaxes(voltages, 0, 1))
    framed0 = lax.all_to_all(frames0, ("yl", "x"), 0, 0, tiled=True)
    framed1 = lax.all_to_all(after(frames1, framed0), ("yl", "x"), 0, 0, tiled=True)
    head0, kept = spectra(framed0, gain[0], tables)
    owned0 = share(after(head0, framed1))
    second = spectra(framed1, gain[1], tables, kept)
    return cross(owned0, share(after(second, owned0)))


def solution(mesh):
    fine = Mesh(mesh.devices.reshape(2, 16, 2, 2, 4), ("yh", "z", "core", "yl", "x"))
    chan, tm = ("yh", "z", "core"), ("yl", "x")
    return jax.shard_map(
        shards,
        mesh=fine,
        in_specs=(P(chan, tm, None), P(chan, None)),
        out_specs=P(None, chan + tm, None, None),
        check_vma=False,
    )
```

```python
import math

import jax
import jax.numpy as jnp
import numpy as np
from jax import lax
from jax.experimental import pallas as pl
from jax.experimental.pallas import tpu as pltpu
from jax.sharding import Mesh, PartitionSpec as P

FFT_LEN = 8192
TAPS = 16
LA = 128
HALF = LA // 2
REF = 32
OUTER = FFT_LEN // LA
SPECTRA = 96
HEAD = 64
TAIL = SPECTRA - HEAD
LEAD = 16
GROUP = 12
VMEM = 40 * 1024 * 1024


def make_tables():
    outer_row = np.arange(OUTER)
    angle_one = 2.0 * np.pi * np.outer(outer_row, outer_row) / OUTER
    first_table = np.concatenate([np.cos(angle_one), -np.sin(angle_one)], axis=1)
    inner_row = np.arange(LA)
    angle_twist = 2.0 * np.pi * np.outer(outer_row, inner_row) / FFT_LEN
    half_row = np.arange(HALF)
    angle_two = 2.0 * np.pi * np.outer(inner_row, half_row) / LA
    upper_rows = np.concatenate([np.cos(angle_two), -np.sin(angle_two)], axis=1)
    lower_rows = np.concatenate([np.sin(angle_two), np.cos(angle_two)], axis=1)
    second_table = np.concatenate([upper_rows, lower_rows], axis=0)
    second_table = second_table.reshape(2 * LA, 2, 2, 16, 2).transpose(0, 1, 3, 2, 4).reshape(2 * LA, 2, HALF)
    second_tables = np.stack([second_table.reshape(2 * LA, LA), second_table[:, ::-1].reshape(2 * LA, LA)])
    sample_pos = np.arange(TAPS * FFT_LEN)
    sinc_arg = np.pi * (sample_pos - TAPS * FFT_LEN / 2 + 0.5) / FFT_LEN
    proto = np.sin(sinc_arg) / sinc_arg
    proto = proto * (0.5 - 0.5 * np.cos(2.0 * np.pi * (sample_pos + 0.5) / (TAPS * FFT_LEN)))
    proto = proto / np.sqrt(np.mean(proto**2) * TAPS)
    taps = proto.reshape(TAPS, FFT_LEN)[::-1].reshape(TAPS, OUTER, LA)
    return (
        jnp.asarray(first_table.T, jnp.float32).astype(jnp.bfloat16),
        jnp.asarray(np.cos(angle_twist), jnp.float32),
        jnp.asarray(np.sin(angle_twist), jnp.float32),
        jnp.asarray(second_tables, jnp.float32).astype(jnp.bfloat16),
        jnp.asarray(taps, jnp.float32),
    )


def frames_kernel(x_ref, o0_ref, o1_ref, wide):
    for n in range(x_ref.shape[0]):
        for b in range(OUTER):
            wide[n, pl.ds(16 * b, 16), :] = x_ref[n, :, b * LA : (b + 1) * LA].astype(jnp.float32)
        for i in range(16):
            out = (o0_ref, o1_ref)[i % 2]
            for h in range(4):
                rows = wide[n, pl.ds(256 * h + i, 16, stride=16), :]
                out[i // 2, n, h * 16 : (h + 1) * 16, :] = rows.astype(jnp.bfloat16)


def to_frames(by_time):
    times, inputs, _ = by_time.shape
    each = 3
    shape = jax.ShapeDtypeStruct((8, times, OUTER, LA), jnp.bfloat16)
    spec = pl.BlockSpec((8, each, OUTER, LA), lambda s: (0, s, 0, 0))
    return pl.pallas_call(
        frames_kernel,
        grid=(times // each,),
        in_specs=[pl.BlockSpec((each, inputs, FFT_LEN), lambda s: (s, 0, 0))],
        out_specs=[spec, spec],
        out_shape=[shape, shape],
        scratch_shapes=[pltpu.VMEM((each, inputs * OUTER, LA), jnp.float32)],
        compiler_params=pltpu.CompilerParams(vmem_limit_bytes=VMEM),
        name="frames",
    )(by_time)


def filter_frames(x_ref, taps_ref, held, filt):
    held[0:LEAD] = jnp.zeros((LEAD, OUTER, LA), jnp.bfloat16)
    for t in range(8):
        held[LEAD + 12 * t : LEAD + 12 * t + 12] = x_ref[t]

    def step(n, carry):
        row = pl.multiple_of((n % 4) * 16, 16)
        base = (n // 4) * GROUP
        acc = [None] * GROUP
        for m in range(GROUP + TAPS - 1):
            v = held[base + (LEAD - TAPS + 1) + m, pl.ds(row, 16), :].astype(jnp.float32)
            for j in range(GROUP):
                p = j + TAPS - 1 - m
                if 0 <= p < TAPS:
                    term = taps_ref[p, pl.ds(row, 16), :] * v
                    acc[j] = term if acc[j] is None else acc[j] + term
        for j in range(GROUP):
            filt[(n // 4) * (GROUP // 4) + j // 4, pl.ds(row, 16), (j % 4) * LA : (j % 4 + 1) * LA] = acc[j].astype(
                jnp.bfloat16
            )
        return carry

    lax.fori_loop(0, 4 * SPECTRA // GROUP, step, 0)


def transform_frames(gain_ref, first_ref, cos_ref, sin_ref, second_ref, filt, spec):
    first = first_ref[...]

    def section_one(g):
        part = jnp.dot(first, filt[g], preferred_element_type=jnp.float32)
        cos = cos_ref[...]
        sin = sin_ref[...]
        rows = []
        for f in range(4):
            u = part[:OUTER, f * LA : (f + 1) * LA]
            v = part[OUTER:, f * LA : (f + 1) * LA]
            rows.append(jnp.concatenate([u * cos + v * sin, v * cos - u * sin], axis=1).astype(jnp.bfloat16))
        return rows

    def section_two(g, rows):
        for h in range(2):
            turned = jnp.concatenate([row[h * 32 : h * 32 + 32] for row in rows], axis=0)
            whole = jnp.dot(turned, second_ref[h], preferred_element_type=jnp.float32)
            gain = gain_ref[h * 32 : h * 32 + 32]
            for f in range(4):
                start = pl.multiple_of((g * 4 + f) * OUTER + h * 32, 32)
                spec[pl.ds(start, 32), :] = whole[f * 32 : f * 32 + 32] * gain

    def step(n, carry):
        earlier = section_one(4 * n)
        for m in range(1, 4):
            later = section_one(4 * n + m)
            section_two(4 * n + m - 1, earlier)
            earlier = later
        section_two(4 * n + 3, earlier)
        return carry

    lax.fori_loop(0, SPECTRA // 16, step, 0)


def turn_spectra(t4, spec, head, tail, tail_row):
    low = lax.broadcasted_iota(jnp.int32, (LA, LA), 1) < HALF
    low_all = lax.broadcasted_iota(jnp.int32, (SPECTRA, LA), 1) < HALF
    low_half = lax.broadcasted_iota(jnp.int32, (HALF, LA), 1) < HALF
    for rp in range(4):
        tails = []
        for kp in range(2):
            k = t4 * 8 + rp * 2 + kp
            one = spec[pl.ds(k, SPECTRA, stride=OUTER), :]
            two = spec[pl.ds(k + 32, SPECTRA, stride=OUTER), :]
            re = jnp.where(low_all, one, two)
            im = jnp.where(low_all, two, one)
            whole = jnp.concatenate([re[:HEAD], im[:HEAD]], axis=0).T
            for k2 in range(2):
                start = (k2 * 8 + rp * 2 + kp) * HALF
                head[start : start + HALF, :] = jnp.where(
                    low_half, whole[k2 * HALF : k2 * HALF + HALF], whole[HALF - k2 * HALF : LA - k2 * HALF]
                )
            tails += [re[HEAD:], im[HEAD:]]
        whole = jnp.concatenate(tails, axis=0).T
        lane = lax.broadcasted_iota(jnp.int32, (HALF, LA), 1)
        real = (lane // TAIL) % 2 == 0
        for k2 in range(2):
            start = (k2 * 8 + tail_row + rp) * HALF
            tail[start : start + HALF, :] = jnp.where(
                real, whole[k2 * HALF : k2 * HALF + HALF], whole[HALF - k2 * HALF : LA - k2 * HALF]
            )


def spread(t4, groups, o_ref, base=0):
    for k2 in range(2):
        for q in range(HALF):
            rows = [group[pl.ds(k2 * 8 * HALF + q, 8, stride=HALF), :] for group in groups]
            o_ref[q // 4, (q % 4) * 8 + k2 * 4 + t4, base : base + 8 * len(groups)] = jnp.concatenate(
                rows, axis=0
            ).astype(jnp.bfloat16)


def spectra_first_kernel(
    x_ref, gain_ref, first_ref, cos_ref, sin_ref, second_ref, taps_ref, head_ref, kept_ref, held, filt, spec, head, tail
):
    filter_frames(x_ref, taps_ref, held, filt)
    transform_frames(gain_ref, first_ref, cos_ref, sin_ref, second_ref, filt, spec)

    def step(t4, carry):
        turn_spectra(t4, spec, head, tail, 0)
        spread(t4, [head], head_ref)
        for k2 in range(2):
            kept_ref[t4, k2] = tail[k2 * 8 * HALF : (k2 * 8 + 4) * HALF, :].astype(jnp.bfloat16)
        return carry

    lax.fori_loop(0, 4, step, 0)


def spectra_second_kernel(
    x_ref, gain_ref, first_ref, cos_ref, sin_ref, second_ref, taps_ref, other_ref, kept_ref, o_ref, held, filt, spec, head, tail
):
    filter_frames(x_ref, taps_ref, held, filt)
    transform_frames(gain_ref, first_ref, cos_ref, sin_ref, second_ref, filt, spec)

    def step(t4, carry):
        turn_spectra(t4, spec, head, tail, 4)
        for k2 in range(2):
            tail[k2 * 8 * HALF : (k2 * 8 + 4) * HALF, :] = kept_ref[t4, k2].astype(jnp.float32)
        spread(t4, [head, tail], o_ref, 8)
        for n in range(4):
            for d in range(32):
                o_ref[4 * t4 + n, d, 0:8] = other_ref[4 * t4 + n, d]
        return carry

    lax.fori_loop(0, 4, step, 0)


def spectra(framed, gain, tables, *kept):
    first = not kept
    out = jax.ShapeDtypeStruct((16, 32, 8 if first else 24, LA), jnp.bfloat16)
    keep = jax.ShapeDtypeStruct((4, 2, 4 * HALF, LA), jnp.bfloat16)
    return pl.pallas_call(
        spectra_first_kernel if first else spectra_second_kernel,
        out_shape=[out, keep] if first else out,
        scratch_shapes=[
            pltpu.VMEM((LEAD + SPECTRA, OUTER, LA), jnp.bfloat16),
            pltpu.VMEM((SPECTRA // 4, OUTER, 4 * LA), jnp.bfloat16),
            pltpu.VMEM((SPECTRA * OUTER, LA), jnp.float32),
            pltpu.VMEM((16 * HALF, LA), jnp.float32),
            pltpu.VMEM((16 * HALF, LA), jnp.float32),
        ],
        compiler_params=pltpu.CompilerParams(vmem_limit_bytes=VMEM),
        cost_estimate=pl.CostEstimate(flops=2_000_000_000, bytes_accessed=4_000_000, transcendentals=0),
        name="spectra_first" if first else "spectra_second",
    )(framed, gain, *tables, *kept)


def cross_kernel(x_ref, o_ref, head, tail):
    def place(z, carry):
        for s in range(32):
            at = (s // 16) * 256 + (s % 16) + z * 16
            head[pl.ds(pl.multiple_of(at * 16, 16), 8), :] = x_ref[z, s, 0:8].astype(jnp.float32)
            head[pl.ds(pl.multiple_of(at * 16 + 8, 8), 8), :] = x_ref[z, s, 8:16].astype(jnp.float32)
            tail[pl.ds(pl.multiple_of(at * 8, 8), 8), :] = x_ref[z, s, 16:24].astype(jnp.float32)
        return carry

    lax.fori_loop(0, 16, place, 0)
    lane = lax.broadcasted_iota(jnp.int32, (REF, LA), 1)
    head_sign = jnp.where(lane < HALF, -1.0, 1.0)
    tail_real = (lane // TAIL) % 2 == 0
    tail_sign = jnp.where(tail_real, -1.0, 1.0)
    for r in range(8):
        mine = lane // HALF == r % 2
        ref_head = head[pl.ds(r, REF, stride=8), :]
        ref_tail = jnp.where(mine, tail[pl.ds(r // 2, REF, stride=4), :], 0.0)
        im_head = pltpu.roll(ref_head, HALF, 1) * head_sign
        im_tail = jnp.where(tail_real, pltpu.roll(ref_tail, LA - TAIL, 1), pltpu.roll(ref_tail, TAIL, 1)) * tail_sign
        weights = jnp.concatenate(
            [jnp.concatenate([ref_head, ref_tail], axis=1), jnp.concatenate([im_head, im_tail], axis=1)], axis=0
        ).astype(jnp.bfloat16)
        for c in range(4):
            rows = jnp.concatenate(
                [
                    head[pl.ds(c * 256 * 8 + r, 256, stride=8), :].astype(jnp.bfloat16),
                    tail[pl.ds(c * 256 * 4 + r // 2, 256, stride=4), :].astype(jnp.bfloat16),
                ],
                axis=1,
            )
            part = lax.dot_general(weights, rows, (((1,), (1,)), ((), ())), preferred_element_type=jnp.float32)
            part = part * (1.0 / SPECTRA)
            for n in range(2):
                o_ref[n, r, :, c * 256 : (c + 1) * 256] = part[n * REF : (n + 1) * REF]


def cross(owned):
    return pl.pallas_call(
        cross_kernel,
        out_shape=jax.ShapeDtypeStruct((2, 8, REF, 1024), jnp.float32),
        scratch_shapes=[pltpu.VMEM((1024 * 8, LA), jnp.float32), pltpu.VMEM((512 * 8, LA), jnp.float32)],
        compiler_params=pltpu.CompilerParams(vmem_limit_bytes=VMEM),
        cost_estimate=pl.CostEstimate(flops=500_000_000, bytes_accessed=5_000_000, transcendentals=0),
        name="cross",
    )(owned)


def share(spec):
    rows = spec.shape[2]
    flat = lax.all_to_all(spec.reshape(512, rows, LA), ("z", "yh", "core", "yl", "x"), 0, 0, tiled=True)
    return flat.reshape(16, 32, rows, LA)


def after(value, other):
    return lax.optimization_barrier((value, other))[0]


def shards(voltages, eq_gain):
    tables = make_tables()
    mine = lax.axis_index("yl") * 4 + lax.axis_index("x")
    gain = lax.dynamic_slice(eq_gain, (2 * mine, 0), (2, eq_gain.shape[1])) * (1.0 / math.sqrt(FFT_LEN))
    gain = gain.reshape(2, 2, 16, 2, OUTER).transpose(0, 4, 2, 1, 3).reshape(2, OUTER, HALF)
    gain = jnp.concatenate([gain, gain], axis=2)
    frames0, frames1 = to_frames(jnp.swapaxes(voltages, 0, 1))
    framed0 = lax.all_to_all(frames0, ("yl", "x"), 0, 0, tiled=True)
    framed1 = lax.all_to_all(after(frames1, framed0), ("yl", "x"), 0, 0, tiled=True)
    head0, kept = spectra(framed0, gain[0], tables)
    return cross(share(spectra(framed1, gain[1], tables, head0, kept)))


def solution(mesh):
    fine = Mesh(mesh.devices.reshape(2, 16, 2, 2, 4), ("yh", "z", "core", "yl", "x"))
    chan, tm = ("yh", "z", "core"), ("yl", "x")
    return jax.shard_map(
        shards,
        mesh=fine,
        in_specs=(P(chan, tm, None), P(chan, None)),
        out_specs=P(None, chan + tm, None, None),
        check_vma=False,
    )
```

```python
import math

import jax
import jax.numpy as jnp
import numpy as np
from jax import lax
from jax.experimental import pallas as pl
from jax.experimental.pallas import tpu as pltpu
from jax.sharding import Mesh, PartitionSpec as P

FFT_LEN = 8192
TAPS = 16
LA = 128
HALF = LA // 2
REF = 32
OUTER = FFT_LEN // LA
SPECTRA = 96
HEAD = 64
TAIL = SPECTRA - HEAD
LEAD = 16
GROUP = 12
EARLY = 32
VMEM = 40 * 1024 * 1024


def make_tables():
    outer_row = np.arange(OUTER)
    angle_one = 2.0 * np.pi * np.outer(outer_row, outer_row) / OUTER
    first_table = np.concatenate([np.cos(angle_one), -np.sin(angle_one)], axis=1)
    inner_row = np.arange(LA)
    angle_twist = 2.0 * np.pi * np.outer(outer_row, inner_row) / FFT_LEN
    half_row = np.arange(HALF)
    angle_two = 2.0 * np.pi * np.outer(inner_row, half_row) / LA
    upper_rows = np.concatenate([np.cos(angle_two), -np.sin(angle_two)], axis=1)
    lower_rows = np.concatenate([np.sin(angle_two), np.cos(angle_two)], axis=1)
    second_table = np.concatenate([upper_rows, lower_rows], axis=0)
    second_table = second_table.reshape(2 * LA, 2, 2, 16, 2).transpose(0, 1, 3, 2, 4).reshape(2 * LA, 2, HALF)
    second_tables = np.stack([second_table.reshape(2 * LA, LA), second_table[:, ::-1].reshape(2 * LA, LA)])
    sample_pos = np.arange(TAPS * FFT_LEN)
    sinc_arg = np.pi * (sample_pos - TAPS * FFT_LEN / 2 + 0.5) / FFT_LEN
    proto = np.sin(sinc_arg) / sinc_arg
    proto = proto * (0.5 - 0.5 * np.cos(2.0 * np.pi * (sample_pos + 0.5) / (TAPS * FFT_LEN)))
    proto = proto / np.sqrt(np.mean(proto**2) * TAPS)
    taps = proto.reshape(TAPS, FFT_LEN)[::-1].reshape(TAPS, OUTER, LA)
    return (
        jnp.asarray(first_table.T, jnp.float32).astype(jnp.bfloat16),
        jnp.asarray(np.cos(angle_twist), jnp.float32),
        jnp.asarray(np.sin(angle_twist), jnp.float32),
        jnp.asarray(second_tables, jnp.float32).astype(jnp.bfloat16),
        jnp.asarray(taps, jnp.float32),
    )


def frames_kernel(x_ref, o0_ref, o1_ref, wide):
    for n in range(x_ref.shape[0]):
        for b in range(OUTER):
            wide[n, pl.ds(16 * b, 16), :] = x_ref[n, :, b * LA : (b + 1) * LA].astype(jnp.float32)
        for i in range(16):
            for h in range(4):
                rows = wide[n, pl.ds(256 * h + i, 16, stride=16), :].astype(jnp.bfloat16)
                at = (i % 2) * 4 + h
                if at < 6:
                    o0_ref[i // 2, n, at * 16 : at * 16 + 16, :] = rows
                else:
                    o1_ref[i // 2, n, at * 16 - 96 : at * 16 - 80, :] = rows


def to_frames(by_time):
    times, inputs, _ = by_time.shape
    each = 3
    spec = lambda rows: pl.BlockSpec((8, each, rows, LA), lambda s: (0, s, 0, 0))
    shape = lambda rows: jax.ShapeDtypeStruct((8, times, rows, LA), jnp.bfloat16)
    return pl.pallas_call(
        frames_kernel,
        grid=(times // each,),
        in_specs=[pl.BlockSpec((each, inputs, FFT_LEN), lambda s: (s, 0, 0))],
        out_specs=[spec(OUTER + EARLY), spec(OUTER - EARLY)],
        out_shape=[shape(OUTER + EARLY), shape(OUTER - EARLY)],
        scratch_shapes=[pltpu.VMEM((each, inputs * OUTER, LA), jnp.float32)],
        compiler_params=pltpu.CompilerParams(vmem_limit_bytes=62 * 1024 * 1024),
        name="frames",
    )(by_time)


def hold_frames(x_ref, held):
    held[0:LEAD] = jnp.zeros((LEAD,) + held.shape[1:], jnp.bfloat16)
    for t in range(8):
        held[LEAD + 12 * t : LEAD + 12 * t + 12] = x_ref[t]


def filter_frames(held, held_row, taps_ref, taps_row, filt, filt_row, rows):
    strips = rows // 16

    def step(n, carry):
        strip = pl.multiple_of((n % strips) * 16, 16)
        group = n // strips
        acc = [None] * GROUP
        for m in range(GROUP + TAPS - 1):
            v = held[group * GROUP + (LEAD - TAPS + 1) + m, pl.ds(held_row + strip, 16), :].astype(jnp.float32)
            for j in range(GROUP):
                p = j + TAPS - 1 - m
                if 0 <= p < TAPS:
                    term = taps_ref[p, pl.ds(taps_row + strip, 16), :] * v
                    acc[j] = term if acc[j] is None else acc[j] + term
        for j in range(GROUP):
            filt[group * (GROUP // 4) + j // 4, pl.ds(filt_row + strip, 16), (j % 4) * LA : (j % 4 + 1) * LA] = acc[
                j
            ].astype(jnp.bfloat16)
        return carry

    lax.fori_loop(0, strips * SPECTRA // GROUP, step, 0)


def transform_frames(gain_ref, first_ref, cos_ref, sin_ref, second_ref, filt, spec):
    first = first_ref[...]

    def section_one(g):
        part = jnp.dot(first, filt[g], preferred_element_type=jnp.float32)
        cos = cos_ref[...]
        sin = sin_ref[...]
        rows = []
        for f in range(4):
            u = part[:OUTER, f * LA : (f + 1) * LA]
            v = part[OUTER:, f * LA : (f + 1) * LA]
            rows.append(jnp.concatenate([u * cos + v * sin, v * cos - u * sin], axis=1).astype(jnp.bfloat16))
        return rows

    def section_two(g, rows):
        for h in range(2):
            turned = jnp.concatenate([row[h * 32 : h * 32 + 32] for row in rows], axis=0)
            whole = jnp.dot(turned, second_ref[h], preferred_element_type=jnp.float32)
            gain = gain_ref[h * 32 : h * 32 + 32]
            for f in range(4):
                start = pl.multiple_of((g * 4 + f) * OUTER + h * 32, 32)
                spec[pl.ds(start, 32), :] = whole[f * 32 : f * 32 + 32] * gain

    def step(n, carry):
        earlier = section_one(4 * n)
        for m in range(1, 4):
            later = section_one(4 * n + m)
            section_two(4 * n + m - 1, earlier)
            earlier = later
        section_two(4 * n + 3, earlier)
        return carry

    lax.fori_loop(0, SPECTRA // 16, step, 0)


def turn_spectra(t4, spec, head, tail, tail_row):
    low = lax.broadcasted_iota(jnp.int32, (LA, LA), 1) < HALF
    low_all = lax.broadcasted_iota(jnp.int32, (SPECTRA, LA), 1) < HALF
    low_half = lax.broadcasted_iota(jnp.int32, (HALF, LA), 1) < HALF
    for rp in range(4):
        tails = []
        for kp in range(2):
            k = t4 * 8 + rp * 2 + kp
            one = spec[pl.ds(k, SPECTRA, stride=OUTER), :]
            two = spec[pl.ds(k + 32, SPECTRA, stride=OUTER), :]
            re = jnp.where(low_all, one, two)
            im = jnp.where(low_all, two, one)
            whole = jnp.concatenate([re[:HEAD], im[:HEAD]], axis=0).T
            for k2 in range(2):
                start = (k2 * 8 + rp * 2 + kp) * HALF
                head[start : start + HALF, :] = jnp.where(
                    low_half, whole[k2 * HALF : k2 * HALF + HALF], whole[HALF - k2 * HALF : LA - k2 * HALF]
                )
            tails += [re[HEAD:], im[HEAD:]]
        whole = jnp.concatenate(tails, axis=0).T
        lane = lax.broadcasted_iota(jnp.int32, (HALF, LA), 1)
        real = (lane // TAIL) % 2 == 0
        for k2 in range(2):
            start = (k2 * 8 + tail_row + rp) * HALF
            tail[start : start + HALF, :] = jnp.where(
                real, whole[k2 * HALF : k2 * HALF + HALF], whole[HALF - k2 * HALF : LA - k2 * HALF]
            )


def spread(t4, groups, o_ref, base=0):
    for k2 in range(2):
        for q in range(HALF):
            rows = [group[pl.ds(k2 * 8 * HALF + q, 8, stride=HALF), :] for group in groups]
            o_ref[q // 4, (q % 4) * 8 + k2 * 4 + t4, base : base + 8 * len(groups)] = jnp.concatenate(
                rows, axis=0
            ).astype(jnp.bfloat16)


def spectra_first_kernel(
    x_ref, gain_ref, first_ref, cos_ref, sin_ref, second_ref, taps_ref,
    head_ref, kept_ref, early_ref, held, filt, spec, head, tail
):
    hold_frames(x_ref, held)
    filter_frames(held, 0, taps_ref, 0, filt, 0, OUTER)
    filter_frames(held, OUTER, taps_ref, 0, early_ref, 0, EARLY)
    transform_frames(gain_ref, first_ref, cos_ref, sin_ref, second_ref, filt, spec)

    def step(t4, carry):
        turn_spectra(t4, spec, head, tail, 0)
        spread(t4, [head], head_ref)
        for k2 in range(2):
            kept_ref[t4, k2] = tail[k2 * 8 * HALF : (k2 * 8 + 4) * HALF, :].astype(jnp.bfloat16)
        return carry

    lax.fori_loop(0, 4, step, 0)


def spectra_second_kernel(
    x_ref, gain_ref, first_ref, cos_ref, sin_ref, second_ref, taps_hbm, other_hbm, kept_hbm, early_hbm,
    o_ref, held, filt, spec, head, tail, taps, other, kept, sems
):
    moves = [
        pltpu.make_async_copy(taps_hbm, taps, sems.at[0]),
        pltpu.make_async_copy(early_hbm, filt.at[:, pl.ds(0, EARLY), :], sems.at[1]),
        pltpu.make_async_copy(other_hbm, other, sems.at[2]),
        pltpu.make_async_copy(kept_hbm, kept, sems.at[3]),
    ]
    for move in moves:
        move.start()
    hold_frames(x_ref, held)
    moves[0].wait()
    filter_frames(held, 0, taps, EARLY, filt, EARLY, OUTER - EARLY)
    for move in moves[1:]:
        move.wait()
    transform_frames(gain_ref, first_ref, cos_ref, sin_ref, second_ref, filt, spec)

    def step(t4, carry):
        turn_spectra(t4, spec, head, tail, 4)
        for k2 in range(2):
            tail[k2 * 8 * HALF : (k2 * 8 + 4) * HALF, :] = kept[t4, k2].astype(jnp.float32)
        spread(t4, [head, tail], o_ref, 8)
        for n in range(4):
            for d in range(32):
                o_ref[4 * t4 + n, d, 0:8] = other[4 * t4 + n, d]
        return carry

    lax.fori_loop(0, 4, step, 0)


HEAD_SHAPE = (16, 32, 8, LA)
KEPT_SHAPE = (4, 2, 4 * HALF, LA)
EARLY_SHAPE = (SPECTRA // 4, EARLY, 4 * LA)


def spectra_scratch(rows):
    return [
        pltpu.VMEM((LEAD + SPECTRA, rows, LA), jnp.bfloat16),
        pltpu.VMEM((SPECTRA // 4, OUTER, 4 * LA), jnp.bfloat16),
        pltpu.VMEM((SPECTRA * OUTER, LA), jnp.float32),
        pltpu.VMEM((16 * HALF, LA), jnp.float32),
        pltpu.VMEM((16 * HALF, LA), jnp.float32),
    ]


def spectra_first(framed, gain, tables):
    return pl.pallas_call(
        spectra_first_kernel,
        out_shape=[jax.ShapeDtypeStruct(shape, jnp.bfloat16) for shape in (HEAD_SHAPE, KEPT_SHAPE, EARLY_SHAPE)],
        scratch_shapes=spectra_scratch(OUTER + EARLY),
        compiler_params=pltpu.CompilerParams(vmem_limit_bytes=VMEM),
        cost_estimate=pl.CostEstimate(flops=2_000_000_000, bytes_accessed=4_000_000, transcendentals=0),
        name="spectra_first",
    )(framed, gain, *tables)


def spectra_second(framed, gain, tables, other, kept, early):
    far = pl.BlockSpec(memory_space=pltpu.HBM)
    near = pl.BlockSpec(memory_space=pltpu.VMEM)
    return pl.pallas_call(
        spectra_second_kernel,
        in_specs=[near] * 6 + [far] * 4,
        out_specs=near,
        out_shape=jax.ShapeDtypeStruct((16, 32, 24, LA), jnp.bfloat16),
        scratch_shapes=spectra_scratch(OUTER - EARLY)
        + [
            pltpu.VMEM((TAPS, OUTER, LA), jnp.float32),
            pltpu.VMEM(HEAD_SHAPE, jnp.bfloat16),
            pltpu.VMEM(KEPT_SHAPE, jnp.bfloat16),
            pltpu.SemaphoreType.DMA((4,)),
        ],
        compiler_params=pltpu.CompilerParams(vmem_limit_bytes=54 * 1024 * 1024),
        cost_estimate=pl.CostEstimate(flops=2_000_000_000, bytes_accessed=4_000_000, transcendentals=0),
        name="spectra_second",
    )(framed, gain, *tables, other, kept, early)


def cross_kernel(x_ref, o_ref, head, tail):
    def place(z, carry):
        for s in range(32):
            at = (s // 16) * 256 + (s % 16) + z * 16
            head[pl.ds(pl.multiple_of(at * 16, 16), 8), :] = x_ref[z, s, 0:8].astype(jnp.float32)
            head[pl.ds(pl.multiple_of(at * 16 + 8, 8), 8), :] = x_ref[z, s, 8:16].astype(jnp.float32)
            tail[pl.ds(pl.multiple_of(at * 8, 8), 8), :] = x_ref[z, s, 16:24].astype(jnp.float32)
        return carry

    lax.fori_loop(0, 16, place, 0)
    lane = lax.broadcasted_iota(jnp.int32, (REF, LA), 1)
    head_sign = jnp.where(lane < HALF, -1.0, 1.0)
    tail_real = (lane // TAIL) % 2 == 0
    tail_sign = jnp.where(tail_real, -1.0, 1.0)
    for r in range(8):
        mine = lane // HALF == r % 2
        ref_head = head[pl.ds(r, REF, stride=8), :]
        ref_tail = jnp.where(mine, tail[pl.ds(r // 2, REF, stride=4), :], 0.0)
        im_head = pltpu.roll(ref_head, HALF, 1) * head_sign
        im_tail = jnp.where(tail_real, pltpu.roll(ref_tail, LA - TAIL, 1), pltpu.roll(ref_tail, TAIL, 1)) * tail_sign
        weights = jnp.concatenate(
            [jnp.concatenate([ref_head, ref_tail], axis=1), jnp.concatenate([im_head, im_tail], axis=1)], axis=0
        ).astype(jnp.bfloat16)
        for c in range(4):
            rows = jnp.concatenate(
                [
                    head[pl.ds(c * 256 * 8 + r, 256, stride=8), :].astype(jnp.bfloat16),
                    tail[pl.ds(c * 256 * 4 + r // 2, 256, stride=4), :].astype(jnp.bfloat16),
                ],
                axis=1,
            )
            part = lax.dot_general(weights, rows, (((1,), (1,)), ((), ())), preferred_element_type=jnp.float32)
            part = part * (1.0 / SPECTRA)
            for n in range(2):
                o_ref[n, r, :, c * 256 : (c + 1) * 256] = part[n * REF : (n + 1) * REF]


def cross(owned):
    return pl.pallas_call(
        cross_kernel,
        out_shape=jax.ShapeDtypeStruct((2, 8, REF, 1024), jnp.float32),
        scratch_shapes=[pltpu.VMEM((1024 * 8, LA), jnp.float32), pltpu.VMEM((512 * 8, LA), jnp.float32)],
        compiler_params=pltpu.CompilerParams(vmem_limit_bytes=VMEM),
        cost_estimate=pl.CostEstimate(flops=500_000_000, bytes_accessed=5_000_000, transcendentals=0),
        name="cross",
    )(owned)


def share(spec):
    rows = spec.shape[2]
    flat = lax.all_to_all(spec.reshape(512, rows, LA), ("z", "yh", "core", "yl", "x"), 0, 0, tiled=True)
    return flat.reshape(16, 32, rows, LA)


def after(value, other):
    return lax.optimization_barrier((value, other))[0]


def shards(voltages, eq_gain):
    tables = make_tables()
    mine = lax.axis_index("yl") * 4 + lax.axis_index("x")
    gain = lax.dynamic_slice(eq_gain, (2 * mine, 0), (2, eq_gain.shape[1])) * (1.0 / math.sqrt(FFT_LEN))
    gain = gain.reshape(2, 2, 16, 2, OUTER).transpose(0, 4, 2, 1, 3).reshape(2, OUTER, HALF)
    gain = jnp.concatenate([gain, gain], axis=2)
    frames0, frames1 = to_frames(jnp.swapaxes(voltages, 0, 1))
    framed0 = lax.all_to_all(frames0, ("yl", "x"), 0, 0, tiled=True)
    framed1 = lax.all_to_all(after(frames1, framed0), ("yl", "x"), 0, 0, tiled=True)
    early = spectra_first(framed0, gain[0], tables)
    return cross(share(spectra_second(framed1, gain[1], tables, *early)))


def solution(mesh):
    fine = Mesh(mesh.devices.reshape(2, 16, 2, 2, 4), ("yh", "z", "core", "yl", "x"))
    chan, tm = ("yh", "z", "core"), ("yl", "x")
    return jax.shard_map(
        shards,
        mesh=fine,
        in_specs=(P(chan, tm, None), P(chan, None)),
        out_specs=P(None, chan + tm, None, None),
        check_vma=False,
    )
```

```python
import math

import jax
import jax.numpy as jnp
import numpy as np
from jax import lax
from jax.experimental import pallas as pl
from jax.experimental.pallas import tpu as pltpu
from jax.sharding import Mesh, PartitionSpec as P

FFT_LEN = 8192
TAPS = 16
LA = 128
HALF = LA // 2
REF = 32
OUTER = FFT_LEN // LA
SPECTRA = 96
HEAD = 64
TAIL = SPECTRA - HEAD
LEAD = 16
GROUP = 12
SPEC_PITCH = 72
ROW_PITCH = 68
WIDE_PITCH = 20
CROSS_PITCH = 12
VMEM = 40 * 1024 * 1024


def make_tables():
    outer_row = np.arange(OUTER)
    angle_one = 2.0 * np.pi * np.outer(outer_row, outer_row) / OUTER
    first_table = np.concatenate([np.cos(angle_one), -np.sin(angle_one)], axis=1)
    inner_row = np.arange(LA)
    angle_twist = 2.0 * np.pi * np.outer(outer_row, inner_row) / FFT_LEN
    half_row = np.arange(HALF)
    angle_two = 2.0 * np.pi * np.outer(inner_row, half_row) / LA
    upper_rows = np.concatenate([np.cos(angle_two), -np.sin(angle_two)], axis=1)
    lower_rows = np.concatenate([np.sin(angle_two), np.cos(angle_two)], axis=1)
    second_table = np.concatenate([upper_rows, lower_rows], axis=0)
    second_table = second_table.reshape(2 * LA, 2, 2, 16, 2).transpose(0, 1, 3, 2, 4).reshape(2 * LA, 2, HALF)
    second_tables = np.stack([second_table.reshape(2 * LA, LA), second_table[:, ::-1].reshape(2 * LA, LA)])
    sample_pos = np.arange(TAPS * FFT_LEN)
    sinc_arg = np.pi * (sample_pos - TAPS * FFT_LEN / 2 + 0.5) / FFT_LEN
    proto = np.sin(sinc_arg) / sinc_arg
    proto = proto * (0.5 - 0.5 * np.cos(2.0 * np.pi * (sample_pos + 0.5) / (TAPS * FFT_LEN)))
    proto = proto / np.sqrt(np.mean(proto**2) * TAPS)
    taps = proto.reshape(TAPS, FFT_LEN)[::-1].reshape(TAPS, OUTER, LA)
    return (
        jnp.asarray(first_table.T, jnp.float32).astype(jnp.bfloat16),
        jnp.asarray(np.cos(angle_twist), jnp.float32),
        jnp.asarray(np.sin(angle_twist), jnp.float32),
        jnp.asarray(second_tables, jnp.float32).astype(jnp.bfloat16),
        jnp.asarray(taps, jnp.float32),
    )


def frames_kernel(x_ref, o0_ref, o1_ref, wide):
    for n in range(x_ref.shape[0]):
        for b in range(OUTER):
            wide[n, pl.ds(WIDE_PITCH * b, 16), :] = x_ref[n, :, b * LA : (b + 1) * LA].astype(jnp.float32)
        for i in range(16):
            out = (o0_ref, o1_ref)[i % 2]
            for h in range(4):
                rows = wide[n, pl.ds(16 * WIDE_PITCH * h + i, 16, stride=WIDE_PITCH), :]
                out[i // 2, n, h * 16 : (h + 1) * 16, :] = rows.astype(jnp.bfloat16)


def to_frames(by_time):
    times, inputs, _ = by_time.shape
    each = 3
    shape = jax.ShapeDtypeStruct((8, times, OUTER, LA), jnp.bfloat16)
    spec = pl.BlockSpec((8, each, OUTER, LA), lambda s: (0, s, 0, 0))
    return pl.pallas_call(
        frames_kernel,
        grid=(times // each,),
        in_specs=[pl.BlockSpec((each, inputs, FFT_LEN), lambda s: (s, 0, 0))],
        out_specs=[spec, spec],
        out_shape=[shape, shape],
        scratch_shapes=[pltpu.VMEM((each, OUTER * WIDE_PITCH, LA), jnp.float32)],
        compiler_params=pltpu.CompilerParams(vmem_limit_bytes=VMEM),
        name="frames",
    )(by_time)


def filter_frames(x_ref, taps_ref, held, filt):
    held[0:LEAD] = jnp.zeros((LEAD, OUTER, LA), jnp.bfloat16)
    for t in range(8):
        held[LEAD + 12 * t : LEAD + 12 * t + 12] = x_ref[t]

    def step(n, carry):
        row = pl.multiple_of((n % 4) * 16, 16)
        base = (n // 4) * GROUP
        acc = [None] * GROUP
        for m in range(GROUP + TAPS - 1):
            v = held[base + (LEAD - TAPS + 1) + m, pl.ds(row, 16), :].astype(jnp.float32)
            for j in range(GROUP):
                p = j + TAPS - 1 - m
                if 0 <= p < TAPS:
                    term = taps_ref[p, pl.ds(row, 16), :] * v
                    acc[j] = term if acc[j] is None else acc[j] + term
        for j in range(GROUP):
            filt[(n // 4) * (GROUP // 4) + j // 4, pl.ds(row, 16), (j % 4) * LA : (j % 4 + 1) * LA] = acc[j].astype(
                jnp.bfloat16
            )
        return carry

    lax.fori_loop(0, 4 * SPECTRA // GROUP, step, 0)


def transform_frames(gain_ref, first_ref, cos_ref, sin_ref, second_ref, filt, spec):
    first = first_ref[...]

    def section_one(g):
        part = jnp.dot(first, filt[g], preferred_element_type=jnp.float32)
        cos = cos_ref[...]
        sin = sin_ref[...]
        rows = []
        for f in range(4):
            u = part[:OUTER, f * LA : (f + 1) * LA]
            v = part[OUTER:, f * LA : (f + 1) * LA]
            rows.append(jnp.concatenate([u * cos + v * sin, v * cos - u * sin], axis=1).astype(jnp.bfloat16))
        return rows

    def section_two(g, rows):
        for h in range(2):
            turned = jnp.concatenate([row[h * 32 : h * 32 + 32] for row in rows], axis=0)
            whole = jnp.dot(turned, second_ref[h], preferred_element_type=jnp.float32)
            gain = gain_ref[h * 32 : h * 32 + 32]
            for f in range(4):
                start = pl.multiple_of((g * 4 + f) * SPEC_PITCH + h * 32, 8)
                spec[pl.ds(start, 32), :] = whole[f * 32 : f * 32 + 32] * gain

    def step(n, carry):
        earlier = section_one(8 * n)
        for m in range(1, 8):
            later = section_one(8 * n + m)
            section_two(8 * n + m - 1, earlier)
            earlier = later
        section_two(8 * n + 7, earlier)
        return carry

    lax.fori_loop(0, SPECTRA // 32, step, 0)


def turn_spectra(t4, spec, head, tail, tail_row):
    low = lax.broadcasted_iota(jnp.int32, (LA, LA), 1) < HALF
    low_all = lax.broadcasted_iota(jnp.int32, (SPECTRA, LA), 1) < HALF
    low_half = lax.broadcasted_iota(jnp.int32, (HALF, LA), 1) < HALF
    for rp in range(4):
        tails = []
        for kp in range(2):
            k = t4 * 8 + rp * 2 + kp
            one = spec[pl.ds(k, SPECTRA, stride=SPEC_PITCH), :]
            two = spec[pl.ds(k + 32, SPECTRA, stride=SPEC_PITCH), :]
            re = jnp.where(low_all, one, two)
            im = jnp.where(low_all, two, one)
            whole = jnp.concatenate([re[:HEAD], im[:HEAD]], axis=0).T
            for k2 in range(2):
                start = (k2 * 8 + rp * 2 + kp) * ROW_PITCH
                head[start : start + HALF, :] = jnp.where(
                    low_half, whole[k2 * HALF : k2 * HALF + HALF], whole[HALF - k2 * HALF : LA - k2 * HALF]
                )
            tails += [re[HEAD:], im[HEAD:]]
        whole = jnp.concatenate(tails, axis=0).T
        lane = lax.broadcasted_iota(jnp.int32, (HALF, LA), 1)
        real = (lane // TAIL) % 2 == 0
        for k2 in range(2):
            start = (k2 * 8 + tail_row + rp) * ROW_PITCH
            tail[start : start + HALF, :] = jnp.where(
                real, whole[k2 * HALF : k2 * HALF + HALF], whole[HALF - k2 * HALF : LA - k2 * HALF]
            )


def spread(t4, groups, o_ref, base=0):
    for k2 in range(2):
        for q in range(HALF):
            rows = [group[pl.ds(k2 * 8 * ROW_PITCH + q, 8, stride=ROW_PITCH), :] for group in groups]
            o_ref[q // 4, (q % 4) * 8 + k2 * 4 + t4, base : base + 8 * len(groups)] = jnp.concatenate(
                rows, axis=0
            ).astype(jnp.bfloat16)


def spectra_first_kernel(
    x_ref, gain_ref, first_ref, cos_ref, sin_ref, second_ref, taps_ref, head_ref, kept_ref, held, filt, spec, head, tail
):
    filter_frames(x_ref, taps_ref, held, filt)
    transform_frames(gain_ref, first_ref, cos_ref, sin_ref, second_ref, filt, spec)

    def step(t4, carry):
        turn_spectra(t4, spec, head, tail, 0)
        spread(t4, [head], head_ref)
        for k2 in range(2):
            for rp in range(4):
                start = (k2 * 8 + rp) * ROW_PITCH
                kept_ref[t4, k2, rp * HALF : rp * HALF + HALF] = tail[start : start + HALF, :].astype(jnp.bfloat16)
        return carry

    lax.fori_loop(0, 4, step, 0)


def spectra_second_kernel(
    x_ref, gain_ref, first_ref, cos_ref, sin_ref, second_ref, taps_ref, other_ref, kept_ref, o_ref, held, filt, spec, head, tail
):
    filter_frames(x_ref, taps_ref, held, filt)
    transform_frames(gain_ref, first_ref, cos_ref, sin_ref, second_ref, filt, spec)

    def step(t4, carry):
        turn_spectra(t4, spec, head, tail, 4)
        for k2 in range(2):
            for rp in range(4):
                start = (k2 * 8 + rp) * ROW_PITCH
                tail[start : start + HALF, :] = kept_ref[t4, k2, rp * HALF : rp * HALF + HALF].astype(jnp.float32)
        spread(t4, [head, tail], o_ref, 8)
        for n in range(4):
            for d in range(32):
                o_ref[4 * t4 + n, d, 0:8] = other_ref[4 * t4 + n, d]
        return carry

    lax.fori_loop(0, 4, step, 0)


def spectra(framed, gain, tables, *kept):
    first = not kept
    out = jax.ShapeDtypeStruct((16, 32, 8 if first else 24, LA), jnp.bfloat16)
    keep = jax.ShapeDtypeStruct((4, 2, 4 * HALF, LA), jnp.bfloat16)
    return pl.pallas_call(
        spectra_first_kernel if first else spectra_second_kernel,
        out_shape=[out, keep] if first else out,
        scratch_shapes=[
            pltpu.VMEM((LEAD + SPECTRA, OUTER, LA), jnp.bfloat16),
            pltpu.VMEM((SPECTRA // 4, OUTER, 4 * LA), jnp.bfloat16),
            pltpu.VMEM((SPECTRA * SPEC_PITCH, LA), jnp.float32),
            pltpu.VMEM((16 * ROW_PITCH, LA), jnp.float32),
            pltpu.VMEM((16 * ROW_PITCH, LA), jnp.float32),
        ],
        compiler_params=pltpu.CompilerParams(vmem_limit_bytes=VMEM),
        cost_estimate=pl.CostEstimate(flops=2_000_000_000, bytes_accessed=4_000_000, transcendentals=0),
        name="spectra_first" if first else "spectra_second",
    )(framed, gain, *tables, *kept)


def cross_kernel(x_ref, o_ref, head, tail):
    def place(z, carry):
        for s in range(32):
            at = (s // 16) * 256 + (s % 16) + z * 16
            head[pl.ds(pl.multiple_of(at * 2 * CROSS_PITCH, 8), 8), :] = x_ref[z, s, 0:8].astype(jnp.float32)
            head[pl.ds(pl.multiple_of(at * 2 * CROSS_PITCH, 8) + CROSS_PITCH, 8), :] = x_ref[z, s, 8:16].astype(jnp.float32)
            tail[pl.ds(pl.multiple_of(at * 8, 8), 8), :] = x_ref[z, s, 16:24].astype(jnp.float32)
        return carry

    lax.fori_loop(0, 16, place, 0)
    lane = lax.broadcasted_iota(jnp.int32, (REF, LA), 1)
    head_sign = jnp.where(lane < HALF, -1.0, 1.0)
    tail_real = (lane // TAIL) % 2 == 0
    tail_sign = jnp.where(tail_real, -1.0, 1.0)
    for r in range(8):
        mine = lane // HALF == r % 2
        ref_head = head[pl.ds(r, REF, stride=CROSS_PITCH), :]
        ref_tail = jnp.where(mine, tail[pl.ds(r // 2, REF, stride=4), :], 0.0)
        im_head = pltpu.roll(ref_head, HALF, 1) * head_sign
        im_tail = jnp.where(tail_real, pltpu.roll(ref_tail, LA - TAIL, 1), pltpu.roll(ref_tail, TAIL, 1)) * tail_sign
        weights = jnp.concatenate(
            [jnp.concatenate([ref_head, ref_tail], axis=1), jnp.concatenate([im_head, im_tail], axis=1)], axis=0
        ).astype(jnp.bfloat16)
        for c in range(4):
            rows = jnp.concatenate(
                [
                    head[pl.ds(c * 256 * CROSS_PITCH + r, 256, stride=CROSS_PITCH), :].astype(jnp.bfloat16),
                    tail[pl.ds(c * 256 * 4 + r // 2, 256, stride=4), :].astype(jnp.bfloat16),
                ],
                axis=1,
            )
            part = lax.dot_general(weights, rows, (((1,), (1,)), ((), ())), preferred_element_type=jnp.float32)
            part = part * (1.0 / SPECTRA)
            for n in range(2):
                o_ref[n, r, :, c * 256 : (c + 1) * 256] = part[n * REF : (n + 1) * REF]


def cross(owned):
    return pl.pallas_call(
        cross_kernel,
        out_shape=jax.ShapeDtypeStruct((2, 8, REF, 1024), jnp.float32),
        scratch_shapes=[pltpu.VMEM((1024 * CROSS_PITCH, LA), jnp.float32), pltpu.VMEM((512 * 8, LA), jnp.float32)],
        compiler_params=pltpu.CompilerParams(vmem_limit_bytes=VMEM),
        cost_estimate=pl.CostEstimate(flops=500_000_000, bytes_accessed=5_000_000, transcendentals=0),
        name="cross",
    )(owned)


def share(spec):
    rows = spec.shape[2]
    flat = lax.all_to_all(spec.reshape(512, rows, LA), ("z", "yh", "core", "yl", "x"), 0, 0, tiled=True)
    return flat.reshape(16, 32, rows, LA)


def after(value, other):
    return lax.optimization_barrier((value, other))[0]


def shards(voltages, eq_gain):
    tables = make_tables()
    mine = lax.axis_index("yl") * 4 + lax.axis_index("x")
    gain = lax.dynamic_slice(eq_gain, (2 * mine, 0), (2, eq_gain.shape[1])) * (1.0 / math.sqrt(FFT_LEN))
    gain = gain.reshape(2, 2, 16, 2, OUTER).transpose(0, 4, 2, 1, 3).reshape(2, OUTER, HALF)
    gain = jnp.concatenate([gain, gain], axis=2)
    frames0, frames1 = to_frames(jnp.swapaxes(voltages, 0, 1))
    framed0 = lax.all_to_all(frames0, ("yl", "x"), 0, 0, tiled=True)
    framed1 = lax.all_to_all(after(frames1, framed0), ("yl", "x"), 0, 0, tiled=True)
    head0, kept = spectra(framed0, gain[0], tables)
    return cross(share(spectra(framed1, gain[1], tables, head0, kept)))


def solution(mesh):
    fine = Mesh(mesh.devices.reshape(2, 16, 2, 2, 4), ("yh", "z", "core", "yl", "x"))
    chan, tm = ("yh", "z", "core"), ("yl", "x")
    return jax.shard_map(
        shards,
        mesh=fine,
        in_specs=(P(chan, tm, None), P(chan, None)),
        out_specs=P(None, chan + tm, None, None),
        check_vma=False,
    )
```

```python
import math

import jax
import jax.numpy as jnp
import numpy as np
from jax import lax
from jax.experimental import pallas as pl
from jax.experimental.pallas import tpu as pltpu
from jax.sharding import Mesh, PartitionSpec as P

FFT_LEN = 8192
TAPS = 16
LA = 128
HALF = LA // 2
REF = 32
OUTER = FFT_LEN // LA
SPECTRA = 96
HEAD = 64
TAIL = SPECTRA - HEAD
LEAD = 16
GROUP = 12
SPEC_PITCH = 72
ROW_PITCH = 68
WIDE_PITCH = 20
CROSS_PITCH = 12
VMEM = 40 * 1024 * 1024


def make_tables():
    outer_row = np.arange(OUTER)
    angle_one = 2.0 * np.pi * np.outer(outer_row, outer_row) / OUTER
    first_table = np.concatenate([np.cos(angle_one), -np.sin(angle_one)], axis=1)
    inner_row = np.arange(LA)
    angle_twist = 2.0 * np.pi * np.outer(outer_row, inner_row) / FFT_LEN
    half_row = np.arange(HALF)
    angle_two = 2.0 * np.pi * np.outer(inner_row, half_row) / LA
    upper_rows = np.concatenate([np.cos(angle_two), -np.sin(angle_two)], axis=1)
    lower_rows = np.concatenate([np.sin(angle_two), np.cos(angle_two)], axis=1)
    second_table = np.concatenate([upper_rows, lower_rows], axis=0)
    second_table = second_table.reshape(2 * LA, 2, 2, 16, 2).transpose(0, 1, 3, 2, 4).reshape(2 * LA, 2, HALF)
    second_tables = np.stack([second_table.reshape(2 * LA, LA), second_table[:, ::-1].reshape(2 * LA, LA)])
    sample_pos = np.arange(TAPS * FFT_LEN)
    sinc_arg = np.pi * (sample_pos - TAPS * FFT_LEN / 2 + 0.5) / FFT_LEN
    proto = np.sin(sinc_arg) / sinc_arg
    proto = proto * (0.5 - 0.5 * np.cos(2.0 * np.pi * (sample_pos + 0.5) / (TAPS * FFT_LEN)))
    proto = proto / np.sqrt(np.mean(proto**2) * TAPS)
    taps = proto.reshape(TAPS, FFT_LEN)[::-1].reshape(TAPS, OUTER, LA)
    return (
        jnp.asarray(first_table.T, jnp.float32).astype(jnp.bfloat16),
        jnp.asarray(np.cos(angle_twist), jnp.float32),
        jnp.asarray(np.sin(angle_twist), jnp.float32),
        jnp.asarray(second_tables, jnp.float32).astype(jnp.bfloat16),
        jnp.asarray(taps, jnp.float32),
    )


def frames_kernel(x_ref, o_ref, wide):
    for n in range(x_ref.shape[0]):
        for b in range(OUTER):
            wide[n, pl.ds(WIDE_PITCH * b, 16), :] = x_ref[n, :, b * LA : (b + 1) * LA].astype(jnp.float32)
        for i in range(16):
            for h in range(4):
                rows = wide[n, pl.ds(16 * WIDE_PITCH * h + i, 16, stride=WIDE_PITCH), :]
                o_ref[i // 2, i % 2, n, h * 16 : (h + 1) * 16, :] = rows.astype(jnp.bfloat16)


def to_frames(by_time):
    times, inputs, _ = by_time.shape
    each = 2
    return pl.pallas_call(
        frames_kernel,
        grid=(times // each,),
        in_specs=[pl.BlockSpec((each, inputs, FFT_LEN), lambda s: (s, 0, 0))],
        out_specs=pl.BlockSpec((8, 2, each, OUTER, LA), lambda s: (0, 0, s, 0, 0)),
        out_shape=jax.ShapeDtypeStruct((8, 2, times, OUTER, LA), jnp.bfloat16),
        scratch_shapes=[pltpu.VMEM((each, OUTER * WIDE_PITCH, LA), jnp.float32)],
        compiler_params=pltpu.CompilerParams(vmem_limit_bytes=62 * 1024 * 1024),
        name="frames",
    )(by_time)


def filter_frames(x_ref, i, taps_ref, held, filt):
    held[0:LEAD] = jnp.zeros((LEAD, OUTER, LA), jnp.bfloat16)
    for t in range(8):
        held[LEAD + 12 * t : LEAD + 12 * t + 12] = x_ref[t, i]

    def step(n, carry):
        row = pl.multiple_of((n % 4) * 16, 16)
        base = (n // 4) * GROUP
        acc = [None] * GROUP
        for m in range(GROUP + TAPS - 1):
            v = held[base + (LEAD - TAPS + 1) + m, pl.ds(row, 16), :].astype(jnp.float32)
            for j in range(GROUP):
                p = j + TAPS - 1 - m
                if 0 <= p < TAPS:
                    term = taps_ref[p, pl.ds(row, 16), :] * v
                    acc[j] = term if acc[j] is None else acc[j] + term
        for j in range(GROUP):
            filt[(n // 4) * (GROUP // 4) + j // 4, pl.ds(row, 16), (j % 4) * LA : (j % 4 + 1) * LA] = acc[j].astype(
                jnp.bfloat16
            )
        return carry

    lax.fori_loop(0, 4 * SPECTRA // GROUP, step, 0)


def transform_frames(i, gain_ref, first_ref, cos_ref, sin_ref, second_ref, filt, spec):
    first = first_ref[...]

    def section_one(g):
        part = jnp.dot(first, filt[g], preferred_element_type=jnp.float32)
        cos = cos_ref[...]
        sin = sin_ref[...]
        rows = []
        for f in range(4):
            u = part[:OUTER, f * LA : (f + 1) * LA]
            v = part[OUTER:, f * LA : (f + 1) * LA]
            rows.append(jnp.concatenate([u * cos + v * sin, v * cos - u * sin], axis=1).astype(jnp.bfloat16))
        return rows

    def section_two(g, rows):
        for h in range(2):
            turned = jnp.concatenate([row[h * 32 : h * 32 + 32] for row in rows], axis=0)
            whole = jnp.dot(turned, second_ref[h], preferred_element_type=jnp.float32)
            gain = gain_ref[i, h * 32 : h * 32 + 32]
            for f in range(4):
                start = pl.multiple_of((g * 4 + f) * SPEC_PITCH + h * 32, 8)
                spec[i, pl.ds(start, 32), :] = whole[f * 32 : f * 32 + 32] * gain

    def step(n, carry):
        earlier = section_one(8 * n)
        for m in range(1, 8):
            later = section_one(8 * n + m)
            section_two(8 * n + m - 1, earlier)
            earlier = later
        section_two(8 * n + 7, earlier)
        return carry

    lax.fori_loop(0, SPECTRA // 32, step, 0)


def turn_spectra(t4, i, spec, head, tail):
    low = lax.broadcasted_iota(jnp.int32, (LA, LA), 1) < HALF
    low_all = lax.broadcasted_iota(jnp.int32, (SPECTRA, LA), 1) < HALF
    low_half = lax.broadcasted_iota(jnp.int32, (HALF, LA), 1) < HALF
    for rp in range(4):
        tails = []
        for kp in range(2):
            k = t4 * 8 + rp * 2 + kp
            one = spec[i, pl.ds(k, SPECTRA, stride=SPEC_PITCH), :]
            two = spec[i, pl.ds(k + 32, SPECTRA, stride=SPEC_PITCH), :]
            re = jnp.where(low_all, one, two)
            im = jnp.where(low_all, two, one)
            whole = jnp.concatenate([re[:HEAD], im[:HEAD]], axis=0).T
            for k2 in range(2):
                start = (k2 * 8 + rp * 2 + kp) * ROW_PITCH
                head[i, start : start + HALF, :] = jnp.where(
                    low_half, whole[k2 * HALF : k2 * HALF + HALF], whole[HALF - k2 * HALF : LA - k2 * HALF]
                )
            tails += [re[HEAD:], im[HEAD:]]
        whole = jnp.concatenate(tails, axis=0).T
        lane = lax.broadcasted_iota(jnp.int32, (HALF, LA), 1)
        real = (lane // TAIL) % 2 == 0
        for k2 in range(2):
            start = (k2 * 8 + i * 4 + rp) * ROW_PITCH
            tail[start : start + HALF, :] = jnp.where(
                real, whole[k2 * HALF : k2 * HALF + HALF], whole[HALF - k2 * HALF : LA - k2 * HALF]
            )


def spread(t4, head, tail, o_ref):
    for k2 in range(2):
        for q in range(HALF):
            at = pl.ds(k2 * 8 * ROW_PITCH + q, 8, stride=ROW_PITCH)
            rows = jnp.concatenate([head[0, at, :], head[1, at, :], tail[at, :]], axis=0)
            o_ref[q // 4, (q % 4) * 8 + k2 * 4 + t4] = rows.astype(jnp.bfloat16)


def spectra_kernel(
    x_ref, gain_ref, first_ref, cos_ref, sin_ref, second_ref, taps_ref, o_ref, held, filt, spec, head, tail
):
    for i in range(2):
        filter_frames(x_ref, i, taps_ref, held, filt)
        transform_frames(i, gain_ref, first_ref, cos_ref, sin_ref, second_ref, filt, spec)

    def step(t4, carry):
        for i in range(2):
            turn_spectra(t4, i, spec, head, tail)
        spread(t4, head, tail, o_ref)
        return carry

    lax.fori_loop(0, 4, step, 0)


def spectra(framed, gain, tables):
    return pl.pallas_call(
        spectra_kernel,
        out_shape=jax.ShapeDtypeStruct((16, 32, 24, LA), jnp.bfloat16),
        scratch_shapes=[
            pltpu.VMEM((LEAD + SPECTRA, OUTER, LA), jnp.bfloat16),
            pltpu.VMEM((SPECTRA // 4, OUTER, 4 * LA), jnp.bfloat16),
            pltpu.VMEM((2, SPECTRA * SPEC_PITCH, LA), jnp.float32),
            pltpu.VMEM((2, 16 * ROW_PITCH, LA), jnp.float32),
            pltpu.VMEM((16 * ROW_PITCH, LA), jnp.float32),
        ],
        compiler_params=pltpu.CompilerParams(vmem_limit_bytes=VMEM),
        name="spectra",
    )(framed, gain, *tables)


def cross_kernel(x_ref, o_ref, head, tail):
    def place(z, carry):
        for s in range(32):
            at = (s // 16) * 256 + (s % 16) + z * 16
            head[pl.ds(pl.multiple_of(at * 2 * CROSS_PITCH, 8), 8), :] = x_ref[z, s, 0:8].astype(jnp.float32)
            head[pl.ds(pl.multiple_of(at * 2 * CROSS_PITCH, 8) + CROSS_PITCH, 8), :] = x_ref[z, s, 8:16].astype(jnp.float32)
            tail[pl.ds(pl.multiple_of(at * 8, 8), 8), :] = x_ref[z, s, 16:24].astype(jnp.float32)
        return carry

    lax.fori_loop(0, 16, place, 0)
    lane = lax.broadcasted_iota(jnp.int32, (REF, LA), 1)
    head_sign = jnp.where(lane < HALF, -1.0, 1.0)
    tail_real = (lane // TAIL) % 2 == 0
    tail_sign = jnp.where(tail_real, -1.0, 1.0)
    for r in range(8):
        mine = lane // HALF == r % 2
        ref_head = head[pl.ds(r, REF, stride=CROSS_PITCH), :]
        ref_tail = jnp.where(mine, tail[pl.ds(r // 2, REF, stride=4), :], 0.0)
        im_head = pltpu.roll(ref_head, HALF, 1) * head_sign
        im_tail = jnp.where(tail_real, pltpu.roll(ref_tail, LA - TAIL, 1), pltpu.roll(ref_tail, TAIL, 1)) * tail_sign
        weights = jnp.concatenate(
            [jnp.concatenate([ref_head, ref_tail], axis=1), jnp.concatenate([im_head, im_tail], axis=1)], axis=0
        ).astype(jnp.bfloat16)
        for c in range(4):
            rows = jnp.concatenate(
                [
                    head[pl.ds(c * 256 * CROSS_PITCH + r, 256, stride=CROSS_PITCH), :].astype(jnp.bfloat16),
                    tail[pl.ds(c * 256 * 4 + r // 2, 256, stride=4), :].astype(jnp.bfloat16),
                ],
                axis=1,
            )
            part = lax.dot_general(weights, rows, (((1,), (1,)), ((), ())), preferred_element_type=jnp.float32)
            part = part * (1.0 / SPECTRA)
            for n in range(2):
                o_ref[n, r, :, c * 256 : (c + 1) * 256] = part[n * REF : (n + 1) * REF]


def cross(owned):
    return pl.pallas_call(
        cross_kernel,
        out_shape=jax.ShapeDtypeStruct((2, 8, REF, 1024), jnp.float32),
        scratch_shapes=[pltpu.VMEM((1024 * CROSS_PITCH, LA), jnp.float32), pltpu.VMEM((512 * 8, LA), jnp.float32)],
        compiler_params=pltpu.CompilerParams(vmem_limit_bytes=VMEM),
        cost_estimate=pl.CostEstimate(flops=500_000_000, bytes_accessed=5_000_000, transcendentals=0),
        name="cross",
    )(owned)


def share(spec):
    rows = spec.shape[2]
    flat = lax.all_to_all(spec.reshape(512, rows, LA), ("z", "yh", "core", "yl", "x"), 0, 0, tiled=True)
    return flat.reshape(16, 32, rows, LA)


def shards(voltages, eq_gain):
    tables = make_tables()
    mine = lax.axis_index("yl") * 4 + lax.axis_index("x")
    gain = lax.dynamic_slice(eq_gain, (2 * mine, 0), (2, eq_gain.shape[1])) * (1.0 / math.sqrt(FFT_LEN))
    gain = gain.reshape(2, 2, 16, 2, OUTER).transpose(0, 4, 2, 1, 3).reshape(2, OUTER, HALF)
    gain = jnp.concatenate([gain, gain], axis=2)
    frames = to_frames(jnp.swapaxes(voltages, 0, 1))
    framed = lax.all_to_all(frames, ("yl", "x"), 0, 0, tiled=True)
    return cross(share(spectra(framed, gain, tables)))


def solution(mesh):
    fine = Mesh(mesh.devices.reshape(2, 16, 2, 2, 4), ("yh", "z", "core", "yl", "x"))
    chan, tm = ("yh", "z", "core"), ("yl", "x")
    return jax.shard_map(
        shards,
        mesh=fine,
        in_specs=(P(chan, tm, None), P(chan, None)),
        out_specs=P(None, chan + tm, None, None),
        check_vma=False,
    )
```
